32 devices in a mesh: groups: 2 (over y), dp: 4 (over z), expert: 4 (over x, core).
Axes of the slice: x: 2, y: 2, z: 4, core: 2. Of those that a mesh axis runs over, the one named last changes fastest.
Arguments:
- tokens: bfloat16 [4096, 4096], P(('groups', 'dp', 'expert')), parts along dimension 0, may hold values from -20 to 20
- cotangent: bfloat16 [4096, 4096], P(('groups', 'dp', 'expert')), parts along dimension 0, may hold values from -24 to 24
- router_weight: bfloat16 [8192, 64], P('groups'), parts along dimension 0, may hold values from -0.0625 to 0.0625
- w_gate: bfloat16 [8192, 16384], P('groups', ('dp', 'expert')), parts along dimension 0, may hold values from -0.09375 to 0.09375
- w_up: bfloat16 [8192, 16384], P('groups', ('dp', 'expert')), parts along dimension 0, may hold values from -0.09375 to 0.09375
- w_down: bfloat16 [32768, 4096], P(('groups', 'dp', 'expert')), parts along dimension 0, may hold values from -0.046875 to 0.046875
- slot_token: int32 [128], P('groups'), parts along dimension 0, may hold values from 0 to 2047, as said below
Outputs:
- d_tokens: bfloat16 [4096, 4096], P(('groups', 'dp', 'expert')), parts along dimension 0
- d_router: float32 [8192, 64], P('groups'), parts along dimension 0
- d_w_gate: bfloat16 [8192, 16384], P('groups', ('dp', 'expert')), parts along dimension 0
- d_w_up: bfloat16 [8192, 16384], P('groups', ('dp', 'expert')), parts along dimension 0
- d_w_down: bfloat16 [32768, 4096], P(('groups', 'dp', 'expert')), parts along dimension 0
The draws below stay inside these ranges and needn't reach their ends.
There are 2 independent parts, one for each index of `groups`. The reference program is written for one: setup_inputs(seed, part) draws one part's arguments, and reference() takes and returns one part's arrays. A program takes and returns all parts, laid end to end along the dimension named above; each array names one. Nothing has to cross between parts.
Inputs may be any that keep to these rules, and one draw needn't show every extreme that they name: `slot_token`: no token fills two slots. The tokens of one device fill at most 6 slots together, and those of some device exactly 6.
All inputs are finite; a program needn't handle non-finite values.
Results may differ from the reference program's by a relative error of at most 0.024.
Values may be sent and summed in bfloat16 or wider, within the bound.
A program may use at most 128 MiB of HBM per device.

```python
import jax
import jax.numpy as jnp

D = 4096
FF = 16384
EXPERTS = 64
TOK_DEV = 128
TOKENS = 2048
CAP = 64
MOST = 6


def shared_router(key):
    raw_values = jax.random.normal(jax.random.fold_in(key, 11), (D, EXPERTS), jnp.float32)
    return jnp.clip(raw_values, -4.0, 4.0) * D ** (-0.5)


def draw_router_weight(key, part):
    return shared_router(key).astype(jnp.bfloat16)


def draw_tokens(key, part):
    key = jax.random.fold_in(key, 2)
    k_base, k_scale, k_dir = jax.random.split(key, 3)
    owner_count = TOKENS // TOK_DEV
    base_rows = jax.random.normal(k_base, (TOKENS, D), jnp.float32)
    row_scale = jnp.exp(jax.random.uniform(k_scale, (TOKENS, 1), jnp.float32, -0.7, 0.7))
    device_id = (jnp.arange(TOKENS) // TOK_DEV).astype(jnp.float32)
    device_ramp = 2.0 * device_id / (owner_count - 1) - 1.0
    direction = jax.random.normal(k_dir, (D,), jnp.float32)
    mixed = base_rows * row_scale + 1.2 * device_ramp[:, None] * direction[None, :]
    return jnp.clip(mixed, -20.0, 20.0).astype(jnp.bfloat16)


def draw_slot_token(key, part):
    key = jax.random.fold_in(key, 5)
    k_shift, k_flip, k_pick, k_order, k_top = jax.random.split(key, 5)
    owner_count = TOKENS // TOK_DEV
    pair_count = owner_count // 2
    mean_load = CAP // owner_count
    spread = MOST - mean_load
    load_shift = jax.random.randint(k_shift, (pair_count,), 0, spread + 1)
    top_pair = jax.random.randint(k_top, (), 0, pair_count)
    load_shift = jnp.where(jnp.arange(pair_count) == top_pair, spread, load_shift)
    flip_pair = jax.random.randint(k_flip, (pair_count,), 0, 2)
    first_load = mean_load + jnp.where(flip_pair == 0, load_shift, -load_shift)
    second_load = 2 * mean_load - first_load
    counts = jnp.stack([first_load, second_load], axis=1).reshape(owner_count)
    pick_keys = jax.random.split(k_pick, owner_count)
    picked = jax.vmap(lambda sub_key: jax.random.permutation(sub_key, TOK_DEV)[:MOST])(pick_keys)
    live_slot = jnp.arange(MOST)[None, :] < counts[:, None]
    global_rows = picked + (jnp.arange(owner_count) * TOK_DEV)[:, None]
    flat_live = live_slot.reshape(-1)
    flat_rows = global_rows.reshape(-1).astype(jnp.int32)
    slot_place = jnp.cumsum(flat_live.astype(jnp.int32)) - 1
    slot_place = jnp.where(flat_live, slot_place, CAP)
    slot_table = jnp.zeros((CAP + 1,), jnp.int32).at[slot_place].set(flat_rows)[:CAP]
    slot_order = jax.random.permutation(k_order, CAP)
    return slot_table[slot_order]


def steps_of(stream_key, dims, cuts, least, top_value):
    gain = 1.0
    for position, blocks in cuts:
        steps = jax.random.uniform(jax.random.fold_in(jax.random.fold_in(stream_key, 6), position), (blocks,), jnp.float32, least / len(cuts), top_value / len(cuts))
        gain = gain * jnp.repeat(jnp.exp(steps), dims[position] // blocks).reshape((-1,) + (1,) * (len(dims) - 1 - position))
    return gain


def gaussian(key, dims, scale, limit, cuts=(), held_as=jnp.bfloat16):
    factor_of = steps_of(key, dims, cuts, -0.22, 0.18) if cuts else 1.0
    result = jax.random.normal(key, dims, jnp.float32) * scale * factor_of
    return jnp.minimum(jnp.maximum(result, -limit), limit).astype(held_as)


def setup_inputs(seed: int = 0, part: int = 0) -> dict:
    arg_keys = jax.random.split(jax.random.key(seed), 8)
    part_keys = jax.random.split(jax.random.fold_in(arg_keys[7], part), 8)
    tokens = draw_tokens(jax.random.fold_in(jax.random.fold_in(arg_keys[7], part), 71), part)
    cotangent = gaussian(part_keys[1], (TOKENS, D), 4.0, 24.0, ((0, 16),))
    router_weight = draw_router_weight(jax.random.fold_in(jax.random.fold_in(arg_keys[7], part), 71), part)
    w_gate = gaussian(part_keys[3], (D, FF), D ** -0.5, 0.09375, ((1, 16),))
    w_up = gaussian(part_keys[4], (D, FF), D ** -0.5, 0.09375, ((1, 16),))
    w_down = gaussian(part_keys[5], (FF, D), FF ** -0.5, 0.046875, ((0, 16),))
    slot_token = draw_slot_token(jax.random.fold_in(jax.random.fold_in(arg_keys[7], part), 71), part)
    return dict(tokens=tokens, cotangent=cotangent, router_weight=router_weight, w_gate=w_gate, w_up=w_up, w_down=w_down, slot_token=slot_token)


balance_weight = 2.0
zloss_weight = 0.3


def reference(tokens, cotangent, router_weight, w_gate, w_up, w_down, slot_token):
    logits = jnp.dot(tokens, router_weight, preferred_element_type=jnp.float32)
    router_probs = jax.nn.softmax(logits, axis=-1)
    log_total = jax.nn.logsumexp(logits, axis=-1)
    gate = router_probs[slot_token, 0]
    chosen = tokens[slot_token]
    chosen_cot = cotangent[slot_token]
    gate_pre = jnp.dot(chosen, w_gate, preferred_element_type=jnp.float32)
    up_pre = jnp.dot(chosen, w_up, preferred_element_type=jnp.float32)
    squash = jax.nn.sigmoid(gate_pre)
    swish = gate_pre * squash
    hidden = (swish * up_pre).astype(jnp.bfloat16)
    down_back = jnp.dot(chosen_cot, w_down.T, preferred_element_type=jnp.float32)
    gate_grad = jnp.sum(hidden.astype(jnp.float32) * down_back, axis=1)
    scaled_cot = (gate[:, None] * chosen_cot.astype(jnp.float32)).astype(jnp.bfloat16)
    d_w_down = jnp.dot(hidden.T, scaled_cot, preferred_element_type=jnp.float32).astype(jnp.bfloat16)
    hidden_grad = gate[:, None] * down_back
    gate_back = (hidden_grad * up_pre * squash * (1.0 + gate_pre * (1.0 - squash))).astype(jnp.bfloat16)
    up_back = (hidden_grad * swish).astype(jnp.bfloat16)
    d_w_gate = jnp.dot(chosen.T, gate_back, preferred_element_type=jnp.float32).astype(jnp.bfloat16)
    d_w_up = jnp.dot(chosen.T, up_back, preferred_element_type=jnp.float32).astype(jnp.bfloat16)
    slot_grad = (jnp.dot(gate_back, w_gate.T, preferred_element_type=jnp.float32)
                 + jnp.dot(up_back, w_up.T, preferred_element_type=jnp.float32)).astype(jnp.bfloat16)
    mean_load = jnp.sum(router_probs, axis=0) / TOKENS
    token_gate = jnp.zeros((TOKENS,), jnp.float32).at[slot_token].add(gate_grad)
    first_column = (jnp.arange(EXPERTS) == 0).astype(jnp.float32)
    prob_grad = 2.0 * balance_weight * EXPERTS * mean_load[None, :] + token_gate[:, None] * first_column[None, :]
    inner_sum = jnp.sum(router_probs * prob_grad, axis=1, keepdims=True)
    logit_grad = router_probs * (prob_grad - inner_sum) + 2.0 * zloss_weight * log_total[:, None] * router_probs
    logit_grad = logit_grad.astype(jnp.bfloat16)
    d_router = jnp.dot(tokens.T, logit_grad, preferred_element_type=jnp.float32)
    routed = jnp.zeros((TOKENS, D), jnp.float32).at[slot_token].add(slot_grad.astype(jnp.float32))
    d_tokens = (routed + jnp.dot(logit_grad, router_weight.T, preferred_element_type=jnp.float32)).astype(jnp.bfloat16)
    return d_tokens, d_router, d_w_gate, d_w_up, d_w_down
```

```python
import functools

import jax
import jax.numpy as jnp
from jax import lax
from jax.experimental import pallas as pl
from jax.experimental.pallas import tpu as pltpu
from jax.sharding import PartitionSpec as P

balance_weight = 2.0
zloss_weight = 0.3


def project_back(gate_rows, up_rows, w_gate, w_up):
    dims = (((1,), (1,)), ((), ()))
    first_part = lax.dot_general(gate_rows, w_gate, dims, preferred_element_type=jnp.float32)
    return first_part + lax.dot_general(up_rows, w_up, dims, preferred_element_type=jnp.float32)


def local(tokens, cotangent, router_weight, w_gate, w_up, w_down, slot_token):
    tok_dev = tokens.shape[0]
    expert_count = router_weight.shape[1]
    owner_count = lax.axis_size(("dp", "expert"))
    my_index = lax.axis_index(("dp", "expert"))
    slot_count = slot_token.shape[0]
    most_rows = 3 * tok_dev // 64
    over_rows = (((0,), (0,)), ((), ()))
    logits = jnp.dot(tokens, router_weight, preferred_element_type=jnp.float32)
    router_probs = jax.nn.softmax(logits, axis=-1)
    log_total = jax.nn.logsumexp(logits, axis=-1)
    column_sums = jnp.sum(router_probs, axis=0)
    load_total = lax.psum(column_sums, ("dp", "expert"))
    owner_dev = slot_token // tok_dev
    local_row = slot_token - owner_dev * tok_dev
    slot_order = jnp.arange(slot_count, dtype=jnp.int32)
    earlier = (owner_dev[None, :] == owner_dev[:, None]) & (
        slot_order[None, :] < slot_order[:, None]
    )
    rank_in = jnp.sum(earlier.astype(jnp.int32), axis=1)
    bucket_row = owner_dev * most_rows + rank_in
    bucket_hit = (owner_dev[None, :] == my_index) & (
        rank_in[None, :] == jnp.arange(most_rows, dtype=jnp.int32)[:, None]
    )
    filled = jnp.any(bucket_hit, axis=1)
    picked = jnp.sum(jnp.where(bucket_hit, local_row[None, :], 0), axis=1)
    my_slot = jnp.sum(jnp.where(bucket_hit, slot_order[None, :], 0), axis=1)
    send_tokens = jnp.where(filled[:, None], tokens[picked], jnp.zeros((), jnp.bfloat16))
    send_cot = jnp.where(filled[:, None], cotangent[picked], jnp.zeros((), jnp.bfloat16))
    send_gate = jnp.where(filled, router_probs[picked, 0], 0.0)
    all_tokens, all_cot, all_gate = (
        lax.all_gather(send_tokens, ("dp", "expert"), axis=0, tiled=True),
        lax.all_gather(send_cot, ("dp", "expert"), axis=0, tiled=True),
        lax.all_gather(send_gate.astype(jnp.bfloat16), ("dp", "expert"), axis=0, tiled=True).astype(
            send_gate.dtype
        ),
    )
    chosen = all_tokens[bucket_row]
    chosen_cot = all_cot[bucket_row]
    gate = all_gate[bucket_row]
    gate_pre = jnp.dot(chosen, w_gate, preferred_element_type=jnp.float32)
    up_pre = jnp.dot(chosen, w_up, preferred_element_type=jnp.float32)
    squash = jax.nn.sigmoid(gate_pre)
    swish = gate_pre * squash
    hidden = (swish * up_pre).astype(jnp.bfloat16)
    down_back = lax.dot_general(
        chosen_cot, w_down, (((1,), (1,)), ((), ())), preferred_element_type=jnp.float32
    )
    gate_part = jnp.sum(hidden.astype(jnp.float32) * down_back, axis=1)
    scaled_cot = (gate[:, None] * chosen_cot.astype(jnp.float32)).astype(jnp.bfloat16)
    d_w_down = lax.dot_general(
        hidden, scaled_cot, over_rows, preferred_element_type=jnp.float32
    ).astype(jnp.bfloat16)
    hidden_grad = gate[:, None] * down_back
    gate_back = (hidden_grad * up_pre * squash * (1.0 + gate_pre * (1.0 - squash))).astype(
        jnp.bfloat16
    )
    up_back = (hidden_grad * swish).astype(jnp.bfloat16)
    d_w_gate = lax.dot_general(
        chosen, gate_back, over_rows, preferred_element_type=jnp.float32
    ).astype(jnp.bfloat16)
    d_w_up = lax.dot_general(chosen, up_back, over_rows, preferred_element_type=jnp.float32).astype(
        jnp.bfloat16
    )
    slot_of = (
        jnp.full((owner_count * most_rows,), slot_count, jnp.int32).at[bucket_row].set(slot_order)
    )
    spare_row = jnp.zeros((1, gate_back.shape[1]), jnp.bfloat16)
    gate_rows = jnp.concatenate([gate_back, spare_row], axis=0)[slot_of]
    up_rows = jnp.concatenate([up_back, spare_row], axis=0)[slot_of]
    returned = lax.psum_scatter(
        project_back(gate_rows, up_rows, w_gate, w_up),
        ("dp", "expert"),
        scatter_dimension=0,
        tiled=True,
    ).astype(jnp.bfloat16)
    gate_total = lax.psum(gate_part, ("dp", "expert"))
    mean_load = load_total / (tok_dev * owner_count)
    bucket_gate = jnp.where(filled, gate_total[my_slot], 0.0)
    scatter_map = (picked[None, :] == jnp.arange(tok_dev, dtype=jnp.int32)[:, None]) & filled[
        None, :
    ]
    token_gate = jnp.sum(jnp.where(scatter_map, bucket_gate[None, :], 0.0), axis=1)
    first_column = (jnp.arange(expert_count) == 0).astype(jnp.float32)
    prob_grad = (
        2.0 * balance_weight * expert_count * mean_load[None, :]
        + token_gate[:, None] * first_column[None, :]
    )
    inner_sum = jnp.sum(router_probs * prob_grad, axis=1, keepdims=True)
    logit_grad = (
        router_probs * (prob_grad - inner_sum)
        + 2.0 * zloss_weight * log_total[:, None] * router_probs
    )
    logit_grad = logit_grad.astype(jnp.bfloat16)
    router_part = lax.dot_general(tokens, logit_grad, over_rows, preferred_element_type=jnp.float32)
    d_router = lax.psum(router_part, ("dp", "expert"))
    routed = jnp.dot(scatter_map.astype(jnp.bfloat16), returned, preferred_element_type=jnp.float32)
    through_router = lax.dot_general(
        logit_grad, router_weight, (((1,), (1,)), ((), ())), preferred_element_type=jnp.float32
    )
    d_tokens = (routed + through_router).astype(jnp.bfloat16)
    return (d_tokens, d_router, d_w_gate, d_w_up, d_w_down)


MESH = pl.DeviceIdType.MESH
f32, bf16 = jnp.float32, jnp.bfloat16
PAD = 8
NT = (((1,), (1,)), ((), ()))
TN = (((0,), (0,)), ((), ()))
HI = lax.Precision.HIGHEST


class Place:
    def __init__(self, nd, ne):
        self.nd, self.nx, self.n = nd, ne // 2, nd * ne
        self.ne = ne
        self.d = lax.axis_index("dp")
        e = lax.axis_index("expert")
        self.x, self.c = e // 2, e % 2
        self.me = self.d * ne + e

    def at(self, d, x, c):
        return {"dp": d, "expert": 2 * x + c}

    def peer(self, offset):
        other = lax.rem(self.me + offset, self.n)
        return other, {"dp": other // self.ne, "expert": lax.rem(other, self.ne)}


def greet(place):
    barrier = pltpu.get_barrier_semaphore()
    for offset in range(1, place.n):
        pl.semaphore_signal(barrier, inc=1, device_id=place.peer(offset)[1], device_id_type=MESH)
    return barrier


def to_all(place, buf, send_sem, recv_sem):
    out = []
    for offset in range(1, place.n):
        _, where = place.peer(offset)
        out.append(
            pltpu.make_async_remote_copy(
                buf.at[place.me], buf.at[place.me], send_sem.at[offset - 1], recv_sem.at[place.me],
                device_id=where, device_id_type=MESH,
            )
        )
    return out


def from_all(place, buf, send_sem, recv_sem):
    for offset in range(1, place.n):
        other, where = place.peer(offset)
        pltpu.make_async_remote_copy(
            buf.at[other], buf.at[other], send_sem.at[offset - 1], recv_sem.at[other],
            device_id=where, device_id_type=MESH,
        ).wait_recv()


def gather_blocks(place, buf, send_sem, recv_sem, mid=None):
    d, x, c, nd = place.d, place.x, place.c, place.nd

    def copy(kind, bd, bx, bc, where):
        block = bd * place.ne + 2 * bx + bc
        return pltpu.make_async_remote_copy(
            buf.at[block], buf.at[block], send_sem.at[kind, block], recv_sem.at[block],
            device_id=where, device_id_type=MESH,
        )

    up = lambda bd: copy(0, bd, x, c, place.at(d + 1, x, c))
    down = lambda bd: copy(0, bd, x, c, place.at(d - 1, x, c))
    across = lambda bd: copy(1, bd, x, c, place.at(d, 1 - x, c))
    sibling = lambda bd, bx: copy(2, bd, bx, c, place.at(d, x, 1 - c))
    up_own = copy(3, d, x, c, place.at(d + 1, x, c))

    @pl.when(d < nd - 1)
    def _():
        up_own.start()

    @pl.when(d > 0)
    def _():
        down(d).start()

    across(d).start()
    sibling(d, x).start()
    if mid is not None:
        mid()

    def arrived(bd, bx, bc):
        copy(0, bd, bx, bc, place.at(d, x, 1 - c)).wait_recv()

    for step in range(1, nd + 1):
        if step < nd:
            low, high = d - step, d + step

            @pl.when(low >= 0)
            def _():
                arrived(low, x, c)

                @pl.when(d < nd - 1)
                def _():
                    up(low).start()

                across(low).start()
                sibling(low, x).start()

            @pl.when(high < nd)
            def _():
                arrived(high, x, c)

                @pl.when(d > 0)
                def _():
                    down(high).start()

                across(high).start()
                sibling(high, x).start()

        low, high = d - (step - 1), d + (step - 1)

        @pl.when(low >= 0)
        def _():
            arrived(low, 1 - x, c)
            sibling(low, 1 - x).start()

        if step > 1:
            @pl.when(high < nd)
            def _():
                arrived(high, 1 - x, c)
                sibling(high, 1 - x).start()

    for bd in range(nd):
        for bx in range(place.nx):
            arrived(bd, bx, 1 - c)

    @pl.when(d < nd - 1)
    def _():
        up_own.wait_send()

    @pl.when(d > 0)
    def _():
        down(d).wait_send()

    for bd in range(nd):
        @pl.when((bd < d) & (d < nd - 1))
        def _():
            up(bd).wait_send()

        @pl.when((bd > d) & (d > 0))
        def _():
            down(bd).wait_send()

        across(bd).wait_send()
        for bx in range(place.nx):
            sibling(bd, bx).wait_send()


def own_slots(slot_row, slot_col, me, tok_dev, row_start, rows):
    slots = slot_row.shape[1]
    local_row = slot_row - me * tok_dev
    hit = ((local_row >= 0) & (local_row < tok_dev)).astype(f32)
    before = (
        lax.broadcasted_iota(jnp.int32, (slots, slots), 0)
        < lax.broadcasted_iota(jnp.int32, (slots, slots), 1)
    ).astype(f32).astype(bf16)
    rank = jnp.dot(jnp.broadcast_to(hit, (8, slots)).astype(bf16), before, preferred_element_type=f32)[:1]
    wanted = (lax.broadcasted_iota(jnp.int32, (rows, slots), 0) - row_start).astype(f32)
    take = jnp.where(wanted == rank, hit, 0.0)
    holds = (lax.broadcasted_iota(jnp.int32, (slots, tok_dev), 1) == slot_col - me * tok_dev).astype(f32)
    return take.astype(bf16), holds.astype(bf16)


def gather_kernel(nd, ne, tok, cot, rw, slot_row, slot_col, rows, probs_out, log_out, load_out,
                  loads, send_sem, recv_sem, load_send, load_recv):
    place = Place(nd, ne)
    barrier = greet(place)
    tok_dev = tok.shape[0]
    take, holds = own_slots(slot_row[...], slot_col[...], place.me, tok_dev, 0, PAD)
    pick = jnp.dot(take, holds, preferred_element_type=f32).astype(bf16)
    width = tok.shape[1] // 4
    for part in range(4):
        cols = pl.ds(part * width, width)
        both = jnp.concatenate(
            [jnp.dot(pick, tok[:, cols], preferred_element_type=f32),
             jnp.dot(pick, cot[:, cols], preferred_element_type=f32)], axis=0)
        rows[place.me, :, cols] = both.astype(bf16)
    pl.semaphore_wait(barrier, place.n - 1)
    sends = to_all(place, loads, load_send, load_recv)

    def mid():
        logits = jnp.dot(tok[...], rw[...], preferred_element_type=f32)
        top = jnp.max(logits, axis=1, keepdims=True)
        raised = jnp.exp(logits - top)
        total = jnp.sum(raised, axis=1, keepdims=True)
        probs = raised / total
        probs_out[...] = probs
        log_out[...] = jnp.log(total) + top
        loads[place.me] = jnp.broadcast_to(jnp.sum(probs, axis=0, keepdims=True), loads.shape[1:])
        for send in sends:
            send.start()

    gather_blocks(place, rows, send_sem, recv_sem, mid)
    from_all(place, loads, load_send, load_recv)
    for send in sends:
        send.wait_send()
    load_out[...] = jnp.sum(loads[...], axis=0)


def expert_kernel(steps, nd, ne, rows, rw, wg, wu, wd, dwg, dwu, dwd, sums, gate_out,
                  ch, cht, ct, sc, gate, acc, part):
    step = pl.program_id(0)
    owners = nd * ne
    slots = owners * PAD
    width = rows.shape[2]

    @pl.when(step == 0)
    def _():
        for pair in range(owners // 2):
            first, second = rows[2 * pair].astype(f32), rows[2 * pair + 1].astype(f32)
            span = pl.ds(pair * 2 * PAD, 2 * PAD)
            ch[span, :] = jnp.concatenate([first[:PAD], second[:PAD]], axis=0).astype(bf16)
            ct[span, :] = jnp.concatenate([first[PAD:], second[PAD:]], axis=0).astype(bf16)
        for k in range(width // 512):
            cht[pl.ds(k * 512, 512), :] = ch[:, pl.ds(k * 512, 512)].T
        logits = jnp.dot(ch[...], rw[...], preferred_element_type=f32)
        raised = jnp.exp(logits - jnp.max(logits, axis=1, keepdims=True))
        probs = raised / jnp.sum(raised, axis=1, keepdims=True)
        gate[...] = probs[:, :1]
        for k in range(width // 512):
            cols = pl.ds(k * 512, 512)
            sc[:, cols] = (gate[...] * ct[:, cols].astype(f32)).astype(bf16)
        acc[...] = jnp.zeros_like(acc)
        part[...] = jnp.zeros_like(part)

    gate_pre = jnp.dot(ch[...], wg[...], preferred_element_type=f32)
    up_pre = jnp.dot(ch[...], wu[...], preferred_element_type=f32)
    down_back = lax.dot_general(ct[...], wd[...], NT, preferred_element_type=f32)
    squash = jax.nn.sigmoid(gate_pre)
    swish = gate_pre * squash
    hidden = (swish * up_pre).astype(bf16)
    part[...] += jnp.sum(hidden.astype(f32) * down_back, axis=1, keepdims=True)
    hidden_grad = gate[...] * down_back
    gate_back = (hidden_grad * up_pre * squash * (1.0 + gate_pre * (1.0 - squash))).astype(bf16)
    up_back = (hidden_grad * swish).astype(bf16)
    hidden_t = hidden.T
    for k in range(width // 512):
        span = pl.ds(k * 512, 512)
        dwd[:, span] = jnp.dot(hidden_t, sc[:, span], preferred_element_type=f32).astype(bf16)
        dwg[span, :] = jnp.dot(cht[span, :], gate_back, preferred_element_type=f32).astype(bf16)
        dwu[span, :] = jnp.dot(cht[span, :], up_back, preferred_element_type=f32).astype(bf16)
        acc[:, span] += lax.dot_general(
            gate_back, wg[span, :], NT, preferred_element_type=f32
        ) + lax.dot_general(up_back, wu[span, :], NT, preferred_element_type=f32)

    @pl.when(step == steps - 1)
    def _():
        for owner in range(owners):
            dd, e = owner // ne, owner % ne
            for k in range(width // 512):
                pair = jnp.concatenate(
                    [acc[pl.ds(owner * PAD, PAD), pl.ds(512 * k, 256)],
                     acc[pl.ds(owner * PAD, PAD), pl.ds(512 * k + 256, 256)]], axis=0)
                sums[e % 2, e // 2, dd, pl.ds(16 * k, 16), :] = pair.astype(bf16)
        gate_out[...] = jnp.broadcast_to(part[...], (slots, slots)).T[:8]


class Scatter:
    def __init__(self, place, src, from_core, one, from_x, two, from_z, sems):
        self.p, self.src = place, src
        self.from_core, self.one, self.from_x, self.two, self.from_z = from_core, one, from_x, two, from_z
        self.cs, self.cr, self.xs, self.xr, self.zs, self.zr = sems
        p = place
        self.core = [
            pltpu.make_async_remote_copy(
                src.at[1 - p.c, bx], from_core.at[bx], self.cs.at[bx], self.cr.at[bx],
                device_id=p.at(p.d, p.x, 1 - p.c), device_id_type=MESH)
            for bx in (1 - p.x, p.x)
        ]
        self.across = [
            pltpu.make_async_remote_copy(
                one.at[bd], from_x.at[bd], self.xs.at[bd], self.xr.at[bd],
                device_id=p.at(p.d, 1 - p.x, p.c), device_id_type=MESH)
            for bd in range(p.nd)
        ]

    def start_core(self):
        for send in self.core:
            send.start()

    def start_across(self):
        p = self.p
        self.core_in(1 - p.x)
        for bd in range(p.nd):
            self.one[bd] = (
                self.src[p.c, 1 - p.x, bd].astype(f32) + self.from_core[1 - p.x, bd].astype(f32)
            ).astype(self.one.dtype)
            self.across[bd].start()
        self.core_in(p.x)

    def core_in(self, bx):
        p = self.p
        pltpu.make_async_remote_copy(
            self.src.at[1 - p.c, bx], self.from_core.at[bx], self.cs.at[bx], self.cr.at[bx],
            device_id=p.at(p.d, p.x, 1 - p.c), device_id_type=MESH).wait_recv()

    def along(self, bd, slot):
        p = self.p
        return pltpu.make_async_remote_copy(
            self.two.at[bd], self.from_z.at[slot], self.zs.at[bd], self.zr.at[slot],
            device_id=p.at(bd, p.x, p.c), device_id_type=MESH)

    def start_along(self):
        p = self.p
        for bd in range(p.nd):
            self.across[bd].wait_recv()
            self.two[bd] = (
                self.src[p.c, p.x, bd].astype(f32) + self.from_core[p.x, bd].astype(f32)
                + self.from_x[bd].astype(f32)
            ).astype(self.two.dtype)

            @pl.when(p.d != bd)
            def _():
                self.along(bd, p.d).start()

    def finish(self):
        p = self.p
        self.from_z[p.d] = self.two[p.d]
        for bd in range(p.nd):
            @pl.when(p.d != bd)
            def _():
                self.along(bd, bd).wait_recv()
        total = self.from_z[0].astype(f32)
        for bd in range(1, p.nd):
            total = total + self.from_z[bd].astype(f32)
        return total

    def drain(self):
        p = self.p
        for send in self.core + self.across:
            send.wait_send()
        for bd in range(p.nd):
            @pl.when(p.d != bd)
            def _():
                self.along(bd, p.d).wait_send()


def combine_kernel(nd, ne, sums, gate_part, tok, rw, probs_in, log_in, load_in, slot_row, slot_col,
                   d_tok, d_rout, gates, rpart, s_core, s_one, s_x, s_two, s_z,
                   r_core, r_one, r_x, r_two, r_z, gate_send, gate_recv,
                   a0, a1, a2, a3, a4, a5, b0, b1, b2, b3, b4, b5, g_send, g_recv):
    place = Place(nd, ne)
    barrier = greet(place)
    me = place.me
    tok_dev, experts = probs_in.shape
    slots = gate_part.shape[1]
    gates[me] = gate_part[...]
    take, holds = own_slots(slot_row[...], slot_col[...], me, tok_dev, 0, PAD)
    take_all, _ = own_slots(slot_row[...], slot_col[...], me, tok_dev, me * PAD, slots)
    tn = (((0,), (1,)), ((), ()))
    place_own = lax.dot_general(holds, take, tn, preferred_element_type=f32).astype(bf16)
    place_all = lax.dot_general(holds, take_all, tn, preferred_element_type=f32)
    pl.semaphore_wait(barrier, place.n - 1)
    rows = Scatter(place, sums, s_core, s_one, s_x, s_two, s_z, (a0, a1, a2, a3, a4, a5))
    rout = Scatter(place, rpart, r_core, r_one, r_x, r_two, r_z, (b0, b1, b2, b3, b4, b5))
    gate_sends = to_all(place, gates, gate_send, gate_recv)
    for send in gate_sends:
        send.start()
    rows.start_core()
    rows.start_across()
    from_all(place, gates, gate_send, gate_recv)
    gate_total = jnp.sum(gates[...], axis=0)[:1]
    token_gate = jnp.sum(place_all * gate_total, axis=1, keepdims=True)
    probs = probs_in[...]
    mean_load = load_in[:1] / (tok_dev * place.n)
    first = (lax.broadcasted_iota(jnp.int32, (1, experts), 1) == 0).astype(f32)
    prob_grad = 2.0 * balance_weight * experts * mean_load + token_gate * first
    inner = jnp.sum(probs * prob_grad, axis=1, keepdims=True)
    lg = probs * (prob_grad - inner) + 2.0 * zloss_weight * log_in[...] * probs
    lg = lg.astype(bf16)
    for owner in range(place.n):
        dd, e = owner // ne, owner % ne
        rpart[e % 2, e // 2, dd] = lax.dot_general(
            lg, tok[:, pl.ds(256 * owner, 256)], TN, preferred_element_type=f32)
    rout.start_core()
    rout.start_across()
    rows.start_along()
    rout.start_along()
    d_rout[me] = rout.finish().astype(bf16)

    def mid():
        returned = rows.finish().astype(bf16).astype(f32)
        for k in range(tok.shape[1] // 256):
            cols = pl.ds(256 * k, 256)
            block = returned[PAD * k:PAD * (k + 1)].astype(bf16)
            d_tok[:, cols] = (
                jnp.dot(place_own, block, preferred_element_type=f32)
                + lax.dot_general(lg, rw[cols, :], NT, preferred_element_type=f32)
            ).astype(bf16)

    gather_blocks(place, d_rout, g_send, g_recv, mid)
    rows.drain()
    rout.drain()
    for send in gate_sends:
        send.wait_send()


def fast_local(nd, ne, tokens, cotangent, router_weight, w_gate, w_up, w_down, slot_token):
    tok_dev, width = tokens.shape
    experts = router_weight.shape[1]
    ff = w_gate.shape[1]
    owners = nd * ne
    slots = owners * PAD
    nx = ne // 2
    slot_row, slot_col = slot_token[None, :], slot_token[:, None]
    vmem = pl.BlockSpec(memory_space=pltpu.VMEM)
    dma = pltpu.SemaphoreType.DMA
    sds = jax.ShapeDtypeStruct
    limit = 56 * 2**20
    rows, probs, log_total, load = pl.pallas_call(
        functools.partial(gather_kernel, nd, ne),
        out_shape=(sds((owners, 2 * PAD, width), bf16), sds((tok_dev, experts), f32),
                   sds((tok_dev, 1), f32), sds((8, experts), f32)),
        in_specs=[vmem] * 5,
        out_specs=(vmem,) * 4,
        scratch_shapes=[pltpu.VMEM((owners, 8, experts), f32), dma((4, owners)), dma((owners,)),
                        dma((owners - 1,)), dma((owners,))],
        compiler_params=pltpu.CompilerParams(
            collective_id=0, has_side_effects=True, vmem_limit_bytes=limit),
    )(tokens, cotangent, router_weight, slot_row, slot_col)

    tile = 256
    steps = ff // tile
    whole = lambda *shape: pl.BlockSpec(shape, lambda i: (0,) * len(shape))
    columns = pl.BlockSpec((width, tile), lambda i: (0, i))
    lines = pl.BlockSpec((tile, width), lambda i: (i, 0))
    d_w_gate, d_w_up, d_w_down, sums, gate_part = pl.pallas_call(
        functools.partial(expert_kernel, steps, nd, ne),
        grid=(steps,),
        out_shape=(sds(w_gate.shape, bf16), sds(w_up.shape, bf16), sds(w_down.shape, bf16),
                   sds((2, nx, nd, PAD * width // 256, 256), bf16), sds((8, slots), f32)),
        in_specs=[whole(owners, 2 * PAD, width), whole(width, experts), columns, columns, lines],
        out_specs=(columns, columns, lines, whole(2, nx, nd, PAD * width // 256, 256), whole(8, slots)),
        scratch_shapes=[pltpu.VMEM((slots, width), bf16), pltpu.VMEM((width, slots), bf16),
                        pltpu.VMEM((slots, width), bf16), pltpu.VMEM((slots, width), bf16),
                        pltpu.VMEM((slots, 1), f32), pltpu.VMEM((slots, width), f32),
                        pltpu.VMEM((slots, 1), f32)],
        compiler_params=pltpu.CompilerParams(vmem_limit_bytes=limit),
    )(rows, router_weight, w_gate, w_up, w_down)

    sblock, rblock = (PAD * width // 256, 256), (experts, 256)

    def stages(block, kind):
        return [pltpu.VMEM((nx, nd) + block, kind), pltpu.VMEM((nd,) + block, kind),
                pltpu.VMEM((nd,) + block, kind), pltpu.VMEM((nd,) + block, kind),
                pltpu.VMEM((nd,) + block, kind)]

    stage_sems = [dma((nx,)), dma((nx,)), dma((nd,)), dma((nd,)), dma((nd,)), dma((nd,))]
    d_tokens, d_rout = pl.pallas_call(
        functools.partial(combine_kernel, nd, ne),
        out_shape=(sds((tok_dev, width), bf16), sds((owners, experts, 256), bf16)),
        in_specs=[vmem] * 9,
        out_specs=(vmem,) * 2,
        scratch_shapes=[pltpu.VMEM((owners, 8, slots), f32), pltpu.VMEM((2, nx, nd) + rblock, f32)]
        + stages(sblock, bf16) + stages(rblock, f32) + [dma((owners - 1,)), dma((owners,))]
        + stage_sems + stage_sems + [dma((4, owners)), dma((owners,))],
        compiler_params=pltpu.CompilerParams(
            collective_id=1, has_side_effects=True, vmem_limit_bytes=limit),
    )(sums, gate_part, tokens, router_weight, probs, log_total, load, slot_row, slot_col)
    d_router = jnp.transpose(d_rout, (0, 2, 1)).reshape(width, experts).astype(f32)
    return d_tokens, d_router, d_w_gate, d_w_up, d_w_down


def solution(mesh):
    placed = (
        P(("groups", "dp", "expert"), None),
        P(("groups", "dp", "expert"), None),
        P("groups", None),
        P("groups", ("dp", "expert")),
        P("groups", ("dp", "expert")),
        P(("groups", "dp", "expert"), None),
        P("groups"),
    )
    nd, ne = mesh.shape["dp"], mesh.shape["expert"]
    body = functools.partial(fast_local, nd, ne) if (nd, ne) == (4, 4) else local
    return jax.shard_map(
        body,
        mesh=mesh,
        in_specs=placed,
        out_specs=(
            P(("groups", "dp", "expert"), None),
            P("groups", None),
            P("groups", ("dp", "expert")),
            P("groups", ("dp", "expert")),
            P(("groups", "dp", "expert"), None),
        ),
        check_vma=False,
    )
```

```python
import functools

import jax
import jax.numpy as jnp
from jax import lax
from jax.experimental import pallas as pl
from jax.experimental.pallas import tpu as pltpu
from jax.sharding import PartitionSpec as P

balance_weight = 2.0
zloss_weight = 0.3


def project_back(gate_rows, up_rows, w_gate, w_up):
    dims = (((1,), (1,)), ((), ()))
    first_part = lax.dot_general(gate_rows, w_gate, dims, preferred_element_type=jnp.float32)
    return first_part + lax.dot_general(up_rows, w_up, dims, preferred_element_type=jnp.float32)


def local(tokens, cotangent, router_weight, w_gate, w_up, w_down, slot_token):
    tok_dev = tokens.shape[0]
    expert_count = router_weight.shape[1]
    owner_count = lax.axis_size(("dp", "expert"))
    my_index = lax.axis_index(("dp", "expert"))
    slot_count = slot_token.shape[0]
    most_rows = 3 * tok_dev // 64
    over_rows = (((0,), (0,)), ((), ()))
    logits = jnp.dot(tokens, router_weight, preferred_element_type=jnp.float32)
    router_probs = jax.nn.softmax(logits, axis=-1)
    log_total = jax.nn.logsumexp(logits, axis=-1)
    column_sums = jnp.sum(router_probs, axis=0)
    load_total = lax.psum(column_sums, ("dp", "expert"))
    owner_dev = slot_token // tok_dev
    local_row = slot_token - owner_dev * tok_dev
    slot_order = jnp.arange(slot_count, dtype=jnp.int32)
    earlier = (owner_dev[None, :] == owner_dev[:, None]) & (
        slot_order[None, :] < slot_order[:, None]
    )
    rank_in = jnp.sum(earlier.astype(jnp.int32), axis=1)
    bucket_row = owner_dev * most_rows + rank_in
    bucket_hit = (owner_dev[None, :] == my_index) & (
        rank_in[None, :] == jnp.arange(most_rows, dtype=jnp.int32)[:, None]
    )
    filled = jnp.any(bucket_hit, axis=1)
    picked = jnp.sum(jnp.where(bucket_hit, local_row[None, :], 0), axis=1)
    my_slot = jnp.sum(jnp.where(bucket_hit, slot_order[None, :], 0), axis=1)
    send_tokens = jnp.where(filled[:, None], tokens[picked], jnp.zeros((), jnp.bfloat16))
    send_cot = jnp.where(filled[:, None], cotangent[picked], jnp.zeros((), jnp.bfloat16))
    send_gate = jnp.where(filled, router_probs[picked, 0], 0.0)
    all_tokens, all_cot, all_gate = (
        lax.all_gather(send_tokens, ("dp", "expert"), axis=0, tiled=True),
        lax.all_gather(send_cot, ("dp", "expert"), axis=0, tiled=True),
        lax.all_gather(send_gate.astype(jnp.bfloat16), ("dp", "expert"), axis=0, tiled=True).astype(
            send_gate.dtype
        ),
    )
    chosen = all_tokens[bucket_row]
    chosen_cot = all_cot[bucket_row]
    gate = all_gate[bucket_row]
    gate_pre = jnp.dot(chosen, w_gate, preferred_element_type=jnp.float32)
    up_pre = jnp.dot(chosen, w_up, preferred_element_type=jnp.float32)
    squash = jax.nn.sigmoid(gate_pre)
    swish = gate_pre * squash
    hidden = (swish * up_pre).astype(jnp.bfloat16)
    down_back = lax.dot_general(
        chosen_cot, w_down, (((1,), (1,)), ((), ())), preferred_element_type=jnp.float32
    )
    gate_part = jnp.sum(hidden.astype(jnp.float32) * down_back, axis=1)
    scaled_cot = (gate[:, None] * chosen_cot.astype(jnp.float32)).astype(jnp.bfloat16)
    d_w_down = lax.dot_general(
        hidden, scaled_cot, over_rows, preferred_element_type=jnp.float32
    ).astype(jnp.bfloat16)
    hidden_grad = gate[:, None] * down_back
    gate_back = (hidden_grad * up_pre * squash * (1.0 + gate_pre * (1.0 - squash))).astype(
        jnp.bfloat16
    )
    up_back = (hidden_grad * swish).astype(jnp.bfloat16)
    d_w_gate = lax.dot_general(
        chosen, gate_back, over_rows, preferred_element_type=jnp.float32
    ).astype(jnp.bfloat16)
    d_w_up = lax.dot_general(chosen, up_back, over_rows, preferred_element_type=jnp.float32).astype(
        jnp.bfloat16
    )
    slot_of = (
        jnp.full((owner_count * most_rows,), slot_count, jnp.int32).at[bucket_row].set(slot_order)
    )
    spare_row = jnp.zeros((1, gate_back.shape[1]), jnp.bfloat16)
    gate_rows = jnp.concatenate([gate_back, spare_row], axis=0)[slot_of]
    up_rows = jnp.concatenate([up_back, spare_row], axis=0)[slot_of]
    returned = lax.psum_scatter(
        project_back(gate_rows, up_rows, w_gate, w_up),
        ("dp", "expert"),
        scatter_dimension=0,
        tiled=True,
    ).astype(jnp.bfloat16)
    gate_total = lax.psum(gate_part, ("dp", "expert"))
    mean_load = load_total / (tok_dev * owner_count)
    bucket_gate = jnp.where(filled, gate_total[my_slot], 0.0)
    scatter_map = (picked[None, :] == jnp.arange(tok_dev, dtype=jnp.int32)[:, None]) & filled[
        None, :
    ]
    token_gate = jnp.sum(jnp.where(scatter_map, bucket_gate[None, :], 0.0), axis=1)
    first_column = (jnp.arange(expert_count) == 0).astype(jnp.float32)
    prob_grad = (
        2.0 * balance_weight * expert_count * mean_load[None, :]
        + token_gate[:, None] * first_column[None, :]
    )
    inner_sum = jnp.sum(router_probs * prob_grad, axis=1, keepdims=True)
    logit_grad = (
        router_probs * (prob_grad - inner_sum)
        + 2.0 * zloss_weight * log_total[:, None] * router_probs
    )
    logit_grad = logit_grad.astype(jnp.bfloat16)
    router_part = lax.dot_general(tokens, logit_grad, over_rows, preferred_element_type=jnp.float32)
    d_router = lax.psum(router_part, ("dp", "expert"))
    routed = jnp.dot(scatter_map.astype(jnp.bfloat16), returned, preferred_element_type=jnp.float32)
    through_router = lax.dot_general(
        logit_grad, router_weight, (((1,), (1,)), ((), ())), preferred_element_type=jnp.float32
    )
    d_tokens = (routed + through_router).astype(jnp.bfloat16)
    return (d_tokens, d_router, d_w_gate, d_w_up, d_w_down)


MESH = pl.DeviceIdType.MESH
f32, bf16 = jnp.float32, jnp.bfloat16
PAD = 8
NT = (((1,), (1,)), ((), ()))
TN = (((0,), (0,)), ((), ()))
HI = lax.Precision.HIGHEST


class Place:
    def __init__(self, nd, ne):
        self.nd, self.nx, self.n = nd, ne // 2, nd * ne
        self.ne = ne
        self.d = lax.axis_index("dp")
        e = lax.axis_index("expert")
        self.x, self.c = e // 2, e % 2
        self.me = self.d * ne + e

    def at(self, d, x, c):
        return {"dp": d, "expert": 2 * x + c}

    def peer(self, offset):
        other = lax.rem(self.me + offset, self.n)
        return other, {"dp": other // self.ne, "expert": lax.rem(other, self.ne)}


def greet(place):
    barrier = pltpu.get_barrier_semaphore()
    for offset in range(1, place.n):
        pl.semaphore_signal(barrier, inc=1, device_id=place.peer(offset)[1], device_id_type=MESH)
    return barrier


def to_all(place, buf, send_sem, recv_sem):
    out = []
    for offset in range(1, place.n):
        _, where = place.peer(offset)
        out.append(
            pltpu.make_async_remote_copy(
                buf.at[place.me], buf.at[place.me], send_sem.at[offset - 1], recv_sem.at[place.me],
                device_id=where, device_id_type=MESH,
            )
        )
    return out


def from_all(place, buf, send_sem, recv_sem):
    for offset in range(1, place.n):
        other, where = place.peer(offset)
        pltpu.make_async_remote_copy(
            buf.at[other], buf.at[other], send_sem.at[offset - 1], recv_sem.at[other],
            device_id=where, device_id_type=MESH,
        ).wait_recv()


def gather_blocks(place, buf, send_sem, recv_sem, mid=None):
    d, x, c, nd = place.d, place.x, place.c, place.nd

    def copy(kind, bd, bx, bc, where):
        block = bd * place.ne + 2 * bx + bc
        return pltpu.make_async_remote_copy(
            buf.at[block], buf.at[block], send_sem.at[kind, block], recv_sem.at[block],
            device_id=where, device_id_type=MESH,
        )

    up = lambda bd: copy(0, bd, x, c, place.at(d + 1, x, c))
    down = lambda bd: copy(0, bd, x, c, place.at(d - 1, x, c))
    across = lambda bd: copy(1, bd, x, c, place.at(d, 1 - x, c))
    sibling = lambda bd, bx: copy(2, bd, bx, c, place.at(d, x, 1 - c))
    up_own = copy(3, d, x, c, place.at(d + 1, x, c))

    @pl.when(d < nd - 1)
    def _():
        up_own.start()

    @pl.when(d > 0)
    def _():
        down(d).start()

    across(d).start()
    sibling(d, x).start()
    if mid is not None:
        mid()

    def arrived(bd, bx, bc):
        copy(0, bd, bx, bc, place.at(d, x, 1 - c)).wait_recv()

    for step in range(1, nd + 1):
        if step < nd:
            low, high = d - step, d + step

            @pl.when(low >= 0)
            def _():
                arrived(low, x, c)

                @pl.when(d < nd - 1)
                def _():
                    up(low).start()

                across(low).start()
                sibling(low, x).start()

            @pl.when(high < nd)
            def _():
                arrived(high, x, c)

                @pl.when(d > 0)
                def _():
                    down(high).start()

                across(high).start()
                sibling(high, x).start()

        low, high = d - (step - 1), d + (step - 1)

        @pl.when(low >= 0)
        def _():
            arrived(low, 1 - x, c)
            sibling(low, 1 - x).start()

        if step > 1:
            @pl.when(high < nd)
            def _():
                arrived(high, 1 - x, c)
                sibling(high, 1 - x).start()

    for bd in range(nd):
        for bx in range(place.nx):
            arrived(bd, bx, 1 - c)

    @pl.when(d < nd - 1)
    def _():
        up_own.wait_send()

    @pl.when(d > 0)
    def _():
        down(d).wait_send()

    for bd in range(nd):
        @pl.when((bd < d) & (d < nd - 1))
        def _():
            up(bd).wait_send()

        @pl.when((bd > d) & (d > 0))
        def _():
            down(bd).wait_send()

        across(bd).wait_send()
        for bx in range(place.nx):
            sibling(bd, bx).wait_send()


def own_slots(slot_row, me, tok_dev, row_start, rows):
    slots = slot_row.shape[1]
    local_row = slot_row - me * tok_dev
    hit = ((local_row >= 0) & (local_row < tok_dev)).astype(f32)
    before = (
        lax.broadcasted_iota(jnp.int32, (slots, slots), 0)
        < lax.broadcasted_iota(jnp.int32, (slots, slots), 1)
    ).astype(f32).astype(bf16)
    rank = jnp.dot(jnp.broadcast_to(hit, (8, slots)).astype(bf16), before, preferred_element_type=f32)[:1]
    wanted = (lax.broadcasted_iota(jnp.int32, (rows, slots), 0) - row_start).astype(f32)
    take = jnp.where(wanted == rank, hit, 0.0)
    holds = (lax.broadcasted_iota(jnp.int32, (tok_dev, slots), 0) == local_row).astype(f32)
    return take.astype(bf16), holds.astype(bf16)


def gather_kernel(nd, ne, tok, cot, rw, slot_row, rows, probs_out, log_out, load_out,
                  loads, send_sem, recv_sem, load_send, load_recv):
    place = Place(nd, ne)
    barrier = greet(place)
    tok_dev = tok.shape[0]
    take, holds = own_slots(slot_row[...], place.me, tok_dev, 0, PAD)
    pick = lax.dot_general(take, holds, NT, preferred_element_type=f32).astype(bf16)
    width = tok.shape[1] // 4
    for part in range(4):
        cols = pl.ds(part * width, width)
        both = jnp.concatenate(
            [jnp.dot(pick, tok[:, cols], preferred_element_type=f32),
             jnp.dot(pick, cot[:, cols], preferred_element_type=f32)], axis=0)
        rows[place.me, :, cols] = both.astype(bf16)
    pl.semaphore_wait(barrier, place.n - 1)
    sends = to_all(place, loads, load_send, load_recv)

    def mid():
        logits = lax.dot_general(tok[...], rw[...], NT, preferred_element_type=f32)
        top = jnp.max(logits, axis=1, keepdims=True)
        raised = jnp.exp(logits - top)
        total = jnp.sum(raised, axis=1, keepdims=True)
        probs = raised / total
        probs_out[...] = probs
        log_out[...] = jnp.log(total) + top
        loads[place.me] = jnp.broadcast_to(jnp.sum(probs, axis=0, keepdims=True), loads.shape[1:])
        for send in sends:
            send.start()

    gather_blocks(place, rows, send_sem, recv_sem, mid)
    from_all(place, loads, load_send, load_recv)
    for send in sends:
        send.wait_send()
    load_out[...] = jnp.sum(loads[...], axis=0)


def expert_kernel(steps, nd, ne, rows, rw, wg, wu, wd, dwg, dwu, dwd, sums, gate_out,
                  ch, cht, ct, sc, gate, acc, part):
    step = pl.program_id(0)
    owners = nd * ne
    slots = owners * PAD
    width = rows.shape[2]

    @pl.when(step == 0)
    def _():
        for pair in range(owners // 2):
            first, second = rows[2 * pair].astype(f32), rows[2 * pair + 1].astype(f32)
            span = pl.ds(pair * 2 * PAD, 2 * PAD)
            ch[span, :] = jnp.concatenate([first[:PAD], second[:PAD]], axis=0).astype(bf16)
            ct[span, :] = jnp.concatenate([first[PAD:], second[PAD:]], axis=0).astype(bf16)
        for k in range(width // 512):
            cht[pl.ds(k * 512, 512), :] = ch[:, pl.ds(k * 512, 512)].T
        logits = lax.dot_general(ch[...], rw[...], NT, preferred_element_type=f32)
        raised = jnp.exp(logits - jnp.max(logits, axis=1, keepdims=True))
        probs = raised / jnp.sum(raised, axis=1, keepdims=True)
        gate[...] = probs[:, :1]
        for k in range(width // 512):
            cols = pl.ds(k * 512, 512)
            sc[:, cols] = (gate[...] * ct[:, cols].astype(f32)).astype(bf16)
        acc[...] = jnp.zeros_like(acc)
        part[...] = jnp.zeros_like(part)

    gate_pre = jnp.dot(ch[...], wg[...], preferred_element_type=f32)
    up_pre = jnp.dot(ch[...], wu[...], preferred_element_type=f32)
    down_back = lax.dot_general(ct[...], wd[...], NT, preferred_element_type=f32)
    squash = jax.nn.sigmoid(gate_pre)
    swish = gate_pre * squash
    hidden = (swish * up_pre).astype(bf16)
    part[...] += jnp.sum(hidden.astype(f32) * down_back, axis=1, keepdims=True)
    hidden_grad = gate[...] * down_back
    gate_back = (hidden_grad * up_pre * squash * (1.0 + gate_pre * (1.0 - squash))).astype(bf16)
    up_back = (hidden_grad * swish).astype(bf16)
    hidden_t = hidden.T
    for k in range(width // 512):
        span = pl.ds(k * 512, 512)
        dwd[:, span] = jnp.dot(hidden_t, sc[:, span], preferred_element_type=f32).astype(bf16)
        dwg[span, :] = jnp.dot(cht[span, :], gate_back, preferred_element_type=f32).astype(bf16)
        dwu[span, :] = jnp.dot(cht[span, :], up_back, preferred_element_type=f32).astype(bf16)
        acc[:, span] += lax.dot_general(
            gate_back, wg[span, :], NT, preferred_element_type=f32
        ) + lax.dot_general(up_back, wu[span, :], NT, preferred_element_type=f32)

    @pl.when(step == steps - 1)
    def _():
        for owner in range(owners):
            dd, e = owner // ne, owner % ne
            for k in range(width // 512):
                pair = jnp.concatenate(
                    [acc[pl.ds(owner * PAD, PAD), pl.ds(512 * k, 256)],
                     acc[pl.ds(owner * PAD, PAD), pl.ds(512 * k + 256, 256)]], axis=0)
                sums[e % 2, e // 2, dd, pl.ds(16 * k, 16), :] = pair.astype(bf16)
        gate_out[...] = jnp.broadcast_to(part[...], (slots, slots)).T[:8]


class Scatter:
    def __init__(self, place, src, from_core, one, from_x, two, from_z, sems):
        self.p, self.src = place, src
        self.from_core, self.one, self.from_x, self.two, self.from_z = from_core, one, from_x, two, from_z
        self.cs, self.cr, self.xs, self.xr, self.zs, self.zr = sems
        p = place
        self.core = [
            pltpu.make_async_remote_copy(
                src.at[1 - p.c, bx], from_core.at[bx], self.cs.at[bx], self.cr.at[bx],
                device_id=p.at(p.d, p.x, 1 - p.c), device_id_type=MESH)
            for bx in (1 - p.x, p.x)
        ]
        self.across = [
            pltpu.make_async_remote_copy(
                one.at[bd], from_x.at[bd], self.xs.at[bd], self.xr.at[bd],
                device_id=p.at(p.d, 1 - p.x, p.c), device_id_type=MESH)
            for bd in range(p.nd)
        ]

    def start_core(self):
        for send in self.core:
            send.start()

    def start_across(self):
        p = self.p
        self.core_in(1 - p.x)
        for bd in range(p.nd):
            self.one[bd] = (
                self.src[p.c, 1 - p.x, bd].astype(f32) + self.from_core[1 - p.x, bd].astype(f32)
            ).astype(self.one.dtype)
            self.across[bd].start()
        self.core_in(p.x)

    def core_in(self, bx):
        p = self.p
        pltpu.make_async_remote_copy(
            self.src.at[1 - p.c, bx], self.from_core.at[bx], self.cs.at[bx], self.cr.at[bx],
            device_id=p.at(p.d, p.x, 1 - p.c), device_id_type=MESH).wait_recv()

    def along(self, bd, slot):
        p = self.p
        return pltpu.make_async_remote_copy(
            self.two.at[bd], self.from_z.at[slot], self.zs.at[bd], self.zr.at[slot],
            device_id=p.at(bd, p.x, p.c), device_id_type=MESH)

    def start_along(self):
        p = self.p
        for bd in range(p.nd):
            self.across[bd].wait_recv()
            self.two[bd] = (
                self.src[p.c, p.x, bd].astype(f32) + self.from_core[p.x, bd].astype(f32)
                + self.from_x[bd].astype(f32)
            ).astype(self.two.dtype)

            @pl.when(p.d != bd)
            def _():
                self.along(bd, p.d).start()

    def finish(self):
        p = self.p
        self.from_z[p.d] = self.two[p.d]
        for bd in range(p.nd):
            @pl.when(p.d != bd)
            def _():
                self.along(bd, bd).wait_recv()
        total = self.from_z[0].astype(f32)
        for bd in range(1, p.nd):
            total = total + self.from_z[bd].astype(f32)
        return total

    def drain(self):
        p = self.p
        for send in self.core + self.across:
            send.wait_send()
        for bd in range(p.nd):
            @pl.when(p.d != bd)
            def _():
                self.along(bd, p.d).wait_send()


def combine_kernel(nd, ne, sums, gate_part, tok, rw, probs_in, log_in, load_in, slot_row,
                   d_tok, d_router_t, d_rout, gates, rpart, s_core, s_one, s_x, s_two, s_z,
                   r_core, r_one, r_x, r_two, r_z, gate_send, gate_recv,
                   a0, a1, a2, a3, a4, a5, b0, b1, b2, b3, b4, b5, g_send, g_recv):
    place = Place(nd, ne)
    barrier = greet(place)
    me = place.me
    tok_dev, experts = probs_in.shape
    slots = gate_part.shape[1]
    gates[me] = gate_part[...]
    take, holds = own_slots(slot_row[...], me, tok_dev, 0, PAD)
    take_all, _ = own_slots(slot_row[...], me, tok_dev, me * PAD, slots)
    place_own = lax.dot_general(holds, take, NT, preferred_element_type=f32).astype(bf16)
    place_all = lax.dot_general(holds, take_all, NT, preferred_element_type=f32)
    pl.semaphore_wait(barrier, place.n - 1)
    rows = Scatter(place, sums, s_core, s_one, s_x, s_two, s_z, (a0, a1, a2, a3, a4, a5))
    rout = Scatter(place, rpart, r_core, r_one, r_x, r_two, r_z, (b0, b1, b2, b3, b4, b5))
    gate_sends = to_all(place, gates, gate_send, gate_recv)
    for send in gate_sends:
        send.start()
    rows.start_core()
    rows.start_across()
    from_all(place, gates, gate_send, gate_recv)
    gate_total = jnp.sum(gates[...], axis=0)[:1]
    token_gate = jnp.sum(place_all * gate_total, axis=1, keepdims=True)
    probs = probs_in[...]
    mean_load = load_in[:1] / (tok_dev * place.n)
    first = (lax.broadcasted_iota(jnp.int32, (1, experts), 1) == 0).astype(f32)
    prob_grad = 2.0 * balance_weight * experts * mean_load + token_gate * first
    inner = jnp.sum(probs * prob_grad, axis=1, keepdims=True)
    lg = probs * (prob_grad - inner) + 2.0 * zloss_weight * log_in[...] * probs
    lg = lg.astype(bf16)
    for owner in range(place.n):
        dd, e = owner // ne, owner % ne
        rpart[e % 2, e // 2, dd] = lax.dot_general(
            lg, tok[:, pl.ds(256 * owner, 256)], TN, preferred_element_type=f32)
    rout.start_core()
    rout.start_across()
    rows.start_along()
    rout.start_along()
    returned = rows.finish().astype(bf16).astype(f32)
    for k in range(tok.shape[1] // 256):
        cols = pl.ds(256 * k, 256)
        block = returned[PAD * k:PAD * (k + 1)].astype(bf16)
        d_tok[:, cols] = (
            jnp.dot(place_own, block, preferred_element_type=f32)
            + jnp.dot(lg, rw[:, cols], preferred_element_type=f32)
        ).astype(bf16)
    d_rout[me] = rout.finish().astype(bf16)
    gather_blocks(place, d_rout, g_send, g_recv)
    for owner in range(place.n):
        d_router_t[:, pl.ds(256 * owner, 256)] = d_rout[owner].astype(f32)
    rows.drain()
    rout.drain()
    for send in gate_sends:
        send.wait_send()


def fast_local(nd, ne, tokens, cotangent, router_weight, w_gate, w_up, w_down, slot_token):
    tok_dev, width = tokens.shape
    experts = router_weight.shape[1]
    ff = w_gate.shape[1]
    router_t = router_weight.T
    owners = nd * ne
    slots = owners * PAD
    nx = ne // 2
    slot_row = slot_token[None, :]
    vmem = pl.BlockSpec(memory_space=pltpu.VMEM)
    dma = pltpu.SemaphoreType.DMA
    sds = jax.ShapeDtypeStruct
    limit = 56 * 2**20
    rows, probs, log_total, load = pl.pallas_call(
        functools.partial(gather_kernel, nd, ne),
        out_shape=(sds((owners, 2 * PAD, width), bf16), sds((tok_dev, experts), f32),
                   sds((tok_dev, 1), f32), sds((8, experts), f32)),
        in_specs=[vmem] * 4,
        out_specs=(vmem,) * 4,
        scratch_shapes=[pltpu.VMEM((owners, 8, experts), f32), dma((4, owners)), dma((owners,)),
                        dma((owners - 1,)), dma((owners,))],
        compiler_params=pltpu.CompilerParams(
            collective_id=0, has_side_effects=True, vmem_limit_bytes=limit),
    )(tokens, cotangent, router_t, slot_row)

    tile = 256
    steps = ff // tile
    whole = lambda *shape: pl.BlockSpec(shape, lambda i: (0,) * len(shape))
    columns = pl.BlockSpec((width, tile), lambda i: (0, i))
    lines = pl.BlockSpec((tile, width), lambda i: (i, 0))
    d_w_gate, d_w_up, d_w_down, sums, gate_part = pl.pallas_call(
        functools.partial(expert_kernel, steps, nd, ne),
        grid=(steps,),
        out_shape=(sds(w_gate.shape, bf16), sds(w_up.shape, bf16), sds(w_down.shape, bf16),
                   sds((2, nx, nd, PAD * width // 256, 256), bf16), sds((8, slots), f32)),
        in_specs=[whole(owners, 2 * PAD, width), whole(experts, width), columns, columns, lines],
        out_specs=(columns, columns, lines, whole(2, nx, nd, PAD * width // 256, 256), whole(8, slots)),
        scratch_shapes=[pltpu.VMEM((slots, width), bf16), pltpu.VMEM((width, slots), bf16),
                        pltpu.VMEM((slots, width), bf16), pltpu.VMEM((slots, width), bf16),
                        pltpu.VMEM((slots, 1), f32), pltpu.VMEM((slots, width), f32),
                        pltpu.VMEM((slots, 1), f32)],
        compiler_params=pltpu.CompilerParams(vmem_limit_bytes=limit),
    )(rows, router_t, w_gate, w_up, w_down)

    sblock, rblock = (PAD * width // 256, 256), (experts, 256)

    def stages(block, kind):
        return [pltpu.VMEM((nx, nd) + block, kind), pltpu.VMEM((nd,) + block, kind),
                pltpu.VMEM((nd,) + block, kind), pltpu.VMEM((nd,) + block, kind),
                pltpu.VMEM((nd,) + block, kind)]

    stage_sems = [dma((nx,)), dma((nx,)), dma((nd,)), dma((nd,)), dma((nd,)), dma((nd,))]
    d_tokens, d_router_t = pl.pallas_call(
        functools.partial(combine_kernel, nd, ne),
        out_shape=(sds((tok_dev, width), bf16), sds((experts, width), f32)),
        in_specs=[vmem] * 8,
        out_specs=(vmem,) * 2,
        scratch_shapes=[pltpu.VMEM((owners, experts, 256), bf16),
                        pltpu.VMEM((owners, 8, slots), f32), pltpu.VMEM((2, nx, nd) + rblock, f32)]
        + stages(sblock, bf16) + stages(rblock, f32) + [dma((owners - 1,)), dma((owners,))]
        + stage_sems + stage_sems + [dma((4, owners)), dma((owners,))],
        compiler_params=pltpu.CompilerParams(
            collective_id=1, has_side_effects=True, vmem_limit_bytes=limit),
    )(sums, gate_part, tokens, router_t, probs, log_total, load, slot_row)
    return d_tokens, d_router_t.T, d_w_gate, d_w_up, d_w_down


def solution(mesh):
    placed = (
        P(("groups", "dp", "expert"), None),
        P(("groups", "dp", "expert"), None),
        P("groups", None),
        P("groups", ("dp", "expert")),
        P("groups", ("dp", "expert")),
        P(("groups", "dp", "expert"), None),
        P("groups"),
    )
    nd, ne = mesh.shape["dp"], mesh.shape["expert"]
    body = functools.partial(fast_local, nd, ne) if (nd, ne) == (4, 4) else local
    return jax.shard_map(
        body,
        mesh=mesh,
        in_specs=placed,
        out_specs=(
            P(("groups", "dp", "expert"), None),
            P("groups", None),
            P("groups", ("dp", "expert")),
            P("groups", ("dp", "expert")),
            P(("groups", "dp", "expert"), None),
        ),
        check_vma=False,
    )
```
